512 devices in a mesh: grp: 16 (over y, x_lo, core), seq: 32 (over z, x_hi).
Axes of the slice: x: 4 (x_hi: 2, x_lo: 2; x = x_hi * 2 + x_lo), y: 4, z: 16, core: 2. Of those that a mesh axis runs over, the one named last changes fastest.
Arguments:
- queries: bfloat16 [16, 4096, 1024], P('grp', 'seq'), may hold values from -8 to 8
- keys: bfloat16 [16, 4096, 1024], P('grp', 'seq'), may hold values from -8 to 8
- values: bfloat16 [16, 4096, 1024], P('grp', 'seq'), may hold values from -6 to 6
- hist_keys: bfloat16 [1024, 1024], P('grp'), may hold values from -6 to 6
- hist_values: bfloat16 [1024, 1024], P('grp'), may hold values from -6 to 6
- lengths: int32 [16], P('grp'), may hold values from 1024 to 4096, as said below
- hist_mask: int32 [16, 8], P('grp'), may hold values 0 or 1
Outputs:
- attended: bfloat16 [16, 4096, 1024], P('grp', 'seq')
The draws below stay inside these ranges and needn't reach their ends.
Inputs may be any that keep to these rules, and one draw needn't show every extreme that they name: `lengths`: some group has all 4096 tokens live and some group only 1024.
All inputs are finite; a program needn't handle non-finite values. No bound on the sum of `hist_mask` on one device may be relied on, other than what follows from the above.
Results may differ from the reference program's by a relative error of at most 0.0043.
Values may be sent and summed in bfloat16 or wider, within the bound.
A program may use at most 64 MiB of HBM per device.

```python
import jax
import jax.numpy as jnp
from jax import lax

HW = 16
HD = 64
HIST = 1024
HBLK = 8
GROUPS = 16
SEQ = 4096
CH = 1024


def draw_queries(key, part):
    key = jax.random.fold_in(key, 1)
    draw = jnp.clip(1.4 * jax.random.normal(key, (GROUPS, SEQ, HW * HD), jnp.float32), -8.0, 8.0)
    return draw.astype(jnp.bfloat16)


def draw_keys(key, part):
    key = jax.random.fold_in(key, 2)
    draw = jnp.clip(jax.random.normal(key, (GROUPS, SEQ, HW * HD), jnp.float32), -8.0, 8.0)
    return draw.astype(jnp.bfloat16)


def draw_lengths(key, part):
    key = jax.random.fold_in(key, 3)
    drawn = jax.random.randint(key, (GROUPS,), SEQ // 4, SEQ + 1)
    fullest = jax.random.randint(jax.random.fold_in(key, 1), (), 0, GROUPS)
    drawn = drawn.at[fullest].set(SEQ)
    return drawn.at[(fullest + 1) % GROUPS].set(SEQ // 4).astype(jnp.int32)


def place_ends(array, key, smallest, top_value):
    dims = array.shape
    spot = [jax.random.randint(jax.random.fold_in(key, axis), (), 0, dims[axis]) for axis in range(len(dims))]
    array = array.at[tuple(spot)].set(smallest)
    longest = dims.index(max(dims))
    spot[longest] = (spot[longest] + 1) % dims[longest]
    return array.at[tuple(spot)].set(top_value)


def block_scale(rng, shape, shards, low, largest):
    factor_of = 1.0
    for position, parts in shards:
        heights = jax.random.uniform(jax.random.fold_in(jax.random.fold_in(rng, 6), position), (parts,), jnp.float32, low / len(shards), largest / len(shards))
        factor_of = factor_of * jnp.repeat(jnp.exp(heights), shape[position] // parts).reshape((-1,) + (1,) * (len(shape) - 1 - position))
    return factor_of


def normal_values(own_key, shape, scale, limit, split=(), kind=jnp.bfloat16):
    result = jax.random.normal(own_key, shape, jnp.float32) * scale
    if len(split) > 0:
        result = block_scale(own_key, shape, split, -0.22, 0.18) * result
    return jnp.clip(result, min=-limit, max=limit).astype(kind)


def setup_inputs(seed: int = 0) -> dict:
    streams_of = jax.random.split(jax.random.key(seed), 8)
    queries = draw_queries(jax.random.fold_in(streams_of[7], 71), 0)
    keys = draw_keys(jax.random.fold_in(streams_of[7], 71), 0)
    values = normal_values(streams_of[2], (GROUPS, SEQ, CH), 1.0, 6.0, ((0, 16), (1, 32)))
    hist_keys = normal_values(streams_of[3], (HIST, CH), 1.0, 6.0, ((0, 16),))
    hist_values = normal_values(streams_of[4], (HIST, CH), 1.0, 6.0, ((0, 16),))
    lengths = draw_lengths(jax.random.fold_in(streams_of[7], 71), 0)
    hist_mask = place_ends((jax.random.randint(streams_of[6], (GROUPS, HBLK), 0, 4) < 3).astype(jnp.int32), jax.random.fold_in(streams_of[6], 1), 0, 1)
    return dict(queries=queries, keys=keys, values=values, hist_keys=hist_keys, hist_values=hist_values, lengths=lengths, hist_mask=hist_mask)


def attend(query_rows, key_rows, value_rows, live):
    count = query_rows.shape[0]
    block = 512 if count % 512 == 0 else count
    blocks = query_rows.reshape(count // block, block, query_rows.shape[1])

    def one_block(rows):
        scores = jnp.dot(rows, key_rows.T, preferred_element_type=jnp.float32) * (HD ** -0.5)
        scores = jnp.where(live[None, :], scores, jnp.float32(-1e30))
        top = jnp.max(scores, axis=1, keepdims=True)
        weights = jnp.where(live[None, :], jnp.exp(scores - top), jnp.float32(0.0))
        total = jnp.sum(weights, axis=1, keepdims=True)
        rounded = weights.astype(jnp.bfloat16)
        mixed = jnp.dot(rounded, value_rows, preferred_element_type=jnp.float32)
        return (mixed / total).astype(jnp.bfloat16)

    return lax.map(one_block, blocks).reshape(count, value_rows.shape[1])


def reference(queries, keys, values, hist_keys, hist_values, lengths, hist_mask):
    positions = jnp.arange(SEQ, dtype=jnp.int32)
    hist_heads_k = hist_keys.reshape(HIST, HW, HD).transpose(1, 0, 2)
    hist_heads_v = hist_values.reshape(HIST, HW, HD).transpose(1, 0, 2)

    def one_group(group_index):
        own_live = positions < lengths[group_index]
        hist_live = jnp.repeat(hist_mask[group_index], HIST // HBLK) > 0
        live = jnp.concatenate([own_live, hist_live])
        group_q = queries[group_index].reshape(SEQ, HW, HD).transpose(1, 0, 2)
        group_k = keys[group_index].reshape(SEQ, HW, HD).transpose(1, 0, 2)
        group_v = values[group_index].reshape(SEQ, HW, HD).transpose(1, 0, 2)

        def one_head(head_index):
            key_rows = jnp.concatenate([group_k[head_index], hist_heads_k[head_index]], axis=0)
            value_rows = jnp.concatenate([group_v[head_index], hist_heads_v[head_index]], axis=0)
            return attend(group_q[head_index], key_rows, value_rows, live)

        heads_out = lax.map(one_head, jnp.arange(HW, dtype=jnp.int32))
        return heads_out.transpose(1, 0, 2).reshape(SEQ, HW * HD)

    return lax.map(one_group, jnp.arange(GROUPS, dtype=jnp.int32))
```

```python
import jax
import jax.numpy as jnp
from jax import lax
from jax.experimental import pallas as pl
from jax.experimental.pallas import tpu as pltpu
from jax.sharding import PartitionSpec as P

HD = 64
HEADS = 16
NZ = 16
TOK = 128
HALF = TOK // 2
SLOTS = 32
HROWS = 64
HIST = 1024
OWN = SLOTS * TOK
KEYS = OWN + HIST
DEAD = -1e30
MESH = pl.DeviceIdType.MESH
BF = jnp.bfloat16


def swap(x):
    return pltpu.roll(x, HD, 1)


def kernel(
    q_hbm, k_hbm, v_hbm, hk_hbm, hv_hbm, len_ref, mask_ref, o_ref,
    q_in, k_in, v_in, hk_in, hv_in,
    kv_src, kv_all, h_src, h_all, q_src, q_all, o_src, o_all,
    k2, v2, s_ref,
    in_sem, kv_ss, kv_rs, x_ss, x_rs, h_ss, h_rs, q_ss, q_rs, o_ss, o_rs,
):
    grp = lax.axis_index("grp")
    seq = lax.axis_index("seq")
    z = seq // 2
    xh = lax.rem(seq, 2)
    hcol = pl.multiple_of(z // 2 * TOK, TOK)
    odd = lax.rem(z, 2)

    loads = [
        pltpu.make_async_copy(k_hbm.at[0], k_in, in_sem.at[0]),
        pltpu.make_async_copy(v_hbm.at[0], v_in, in_sem.at[1]),
        pltpu.make_async_copy(hk_hbm.at[:, pl.ds(hcol, TOK)], hk_in, in_sem.at[2]),
        pltpu.make_async_copy(hv_hbm.at[:, pl.ds(hcol, TOK)], hv_in, in_sem.at[3]),
        pltpu.make_async_copy(q_hbm.at[0], q_in, in_sem.at[4]),
    ]
    for load in loads:
        load.start()

    def z_peer(t):
        return {"seq": t * 2 + xh}

    barrier = pltpu.get_barrier_semaphore()

    def far(i):
        return lax.rem(z + 8 + (1 - 2 * lax.rem(i, 2)) * ((i + 1) // 2), NZ)

    def greet_z(i, c):
        pl.semaphore_signal(barrier, inc=1, device_id=z_peer(far(i)), device_id_type=MESH)
        return c

    lax.fori_loop(0, NZ - 1, greet_z, 0)
    pl.semaphore_signal(barrier, inc=1, device_id={"seq": z * 2 + 1 - xh}, device_id_type=MESH)

    def greet_g(i, c):
        pl.semaphore_signal(barrier, inc=1, device_id={"grp": lax.rem(grp + i, 16)}, device_id_type=MESH)
        return c

    lax.fori_loop(1, 16, greet_g, 0)

    def lane(rows):
        return lax.broadcasted_iota(jnp.int32, (rows, TOK), 1)

    low = lane(TOK) < HD
    low_half = lane(HALF) < HD

    loads[0].wait()
    loads[1].wait()
    for c in range(HEADS // 2):
        kk = k_in[:, c * TOK : (c + 1) * TOK]
        vv = v_in[:, c * TOK : (c + 1) * TOK]
        kv_src[2 * c] = jnp.where(low, kk, swap(vv))
        kv_src[2 * c + 1] = jnp.where(low, swap(kk), vv)
    loads[2].wait()
    loads[3].wait()
    hk = hk_in[...]
    hv = hv_in[...]
    even_h = jnp.where(low_half, hk, swap(hv))
    odd_h = jnp.where(low_half, swap(hk), hv)
    pick = jnp.full((HROWS, TOK), odd, jnp.int32) == 1
    h_src[...] = jnp.where(pick, odd_h, even_h)

    pl.semaphore_wait(barrier, 31)

    def kv_copy(t, slot):
        return pltpu.make_async_remote_copy(
            src_ref=kv_src.at[t], dst_ref=kv_all.at[slot * 2 + xh],
            send_sem=kv_ss.at[t], recv_sem=kv_rs.at[slot],
            device_id=z_peer(t), device_id_type=MESH,
        )

    def x_copy(t, side):
        return pltpu.make_async_remote_copy(
            src_ref=kv_all.at[t * 2 + side], dst_ref=kv_all.at[t * 2 + side],
            send_sem=x_ss.at[t], recv_sem=x_rs.at[t],
            device_id={"seq": z * 2 + 1 - xh}, device_id_type=MESH,
        )

    def h_copy(t, slot):
        return pltpu.make_async_remote_copy(
            src_ref=h_src, dst_ref=h_all.at[slot],
            send_sem=h_ss.at[t], recv_sem=h_rs.at[slot],
            device_id={"grp": t}, device_id_type=MESH,
        )

    def q_copy(t, slot):
        return pltpu.make_async_remote_copy(
            src_ref=q_src.at[t], dst_ref=q_all.at[slot],
            send_sem=q_ss.at[t], recv_sem=q_rs.at[slot],
            device_id=z_peer(t), device_id_type=MESH,
        )

    def o_copy(t, slot):
        return pltpu.make_async_remote_copy(
            src_ref=o_src.at[t], dst_ref=o_all.at[slot],
            send_sem=o_ss.at[t], recv_sem=o_rs.at[slot],
            device_id=z_peer(t), device_id_type=MESH,
        )

    def loop(lo, hi, f):
        def step(i, c):
            f(i)
            return c

        lax.fori_loop(lo, hi, step, 0)

    loop(0, NZ - 1, lambda i: kv_copy(far(i), z).start())
    kv_all[z * 2 + xh] = kv_src[z]
    x_copy(z, xh).start()
    loop(1, 16, lambda i: h_copy(lax.rem(grp + i, 16), grp).start())

    loads[4].wait()
    scale = jnp.asarray(HD**-0.5, BF)
    for c in range(HEADS // 2):
        qq = q_in[:, c * TOK : (c + 1) * TOK] * scale
        top, bot = qq[:HALF], qq[HALF:]
        q_src[2 * c] = jnp.where(low_half, top, swap(bot))
        q_src[2 * c + 1] = jnp.where(low_half, swap(top), bot)
    loop(0, NZ - 1, lambda i: q_copy(far(i), z).start())
    q_all[z] = q_src[z]

    length = len_ref[0]

    def place(kv, rows, at, live):
        column = lane(rows)
        bias = jnp.where(live, 0.0, DEAD).astype(BF)
        k2[pl.ds(at, rows), :] = jnp.where(column < HD, kv, jnp.where(column == HD, bias, jnp.zeros_like(bias)))
        ones = jnp.where(column == HD, 1.0, 0.0).astype(BF)
        v2[pl.ds(at, rows), :] = jnp.where(column < HD, swap(kv), ones)

    def place_own(slot):
        at = pl.multiple_of(slot * TOK, TOK)
        pos = slot * TOK + lax.broadcasted_iota(jnp.int32, (TOK, TOK), 0)
        place(kv_all[slot], TOK, at, pos < length)

    place_own(z * 2 + xh)

    def on_kv(i):
        t = far(i)
        kv_copy(t, t).wait_recv()
        x_copy(t, xh).start()
        place_own(t * 2 + xh)

    loop(0, NZ - 1, on_kv)

    h_all[grp] = h_src[...]
    loop(1, 16, lambda i: h_copy(lax.rem(grp + i, 16), lax.rem(grp + i, 16)).wait_recv())
    for b in range(16):
        flag = jnp.full((HROWS, TOK), mask_ref[0, b // 2], jnp.int32) > 0
        place(h_all[b], HROWS, OWN + b * HROWS, flag)

    x_copy(z, 1 - xh).wait_recv()
    place_own(z * 2 + 1 - xh)

    def on_x(i):
        t = far(i)
        x_copy(t, 1 - xh).wait_recv()
        place_own(t * 2 + 1 - xh)

    loop(0, NZ - 1, on_x)

    def open_q(t):
        packed = q_all[t]
        one = jnp.where(lane(HALF) == HD, 1.0, 0.0).astype(BF)
        return [jnp.where(low_half, packed, one), jnp.where(low_half, swap(packed), one)]

    def close_o(rows):
        return jnp.where(low_half, rows[:HALF], swap(rows[HALF:]))

    rows = 2 * TOK
    chunk = 1024

    def attend(j):
        first = lax.rem(z + 8 + j, NZ)
        second = lax.rem(z + 8 - j + NZ, NZ)
        second = jnp.where(j == 0, z, second)
        q_copy(first, first).wait_recv()

        @pl.when(j != 0)
        def _():
            q_copy(second, second).wait_recv()

        q2 = jnp.concatenate(open_q(first) + open_q(second), axis=0)
        best = jnp.full((rows, TOK), -jnp.inf, jnp.float32)
        for c in range(0, KEYS, chunk):
            scores = lax.dot_general(
                q2, k2[c : c + chunk, :], (((1,), (1,)), ((), ())), preferred_element_type=jnp.float32
            )
            s_ref[:, c : c + chunk] = scores
            for n in range(0, chunk, TOK):
                best = jnp.maximum(best, scores[:, n : n + TOK])
        top = jnp.max(best, axis=1, keepdims=True)
        mixed = jnp.zeros((rows, TOK), jnp.float32)
        for c in range(0, KEYS, chunk):
            weights = jnp.exp(s_ref[:, c : c + chunk] - top).astype(BF)
            mixed += jnp.dot(weights, v2[c : c + chunk, :], preferred_element_type=jnp.float32)
        out = (mixed / mixed[:, HD : HD + 1]).astype(BF)
        o_src[first] = close_o(out[:TOK])
        o_copy(first, z).start()

        @pl.when(j == 0)
        def _():
            o_all[z] = close_o(out[TOK:])

        @pl.when(j != 0)
        def _():
            o_src[second] = close_o(out[TOK:])
            o_copy(second, z).start()

    loop(0, 8, attend)

    loop(0, NZ - 1, lambda i: o_copy(far(i), far(i)).wait_recv())
    for c in range(HEADS // 2):
        a, b = o_all[2 * c], o_all[2 * c + 1]
        cols = slice(c * TOK, (c + 1) * TOK)
        o_ref[0, :HALF, cols] = jnp.where(low_half, a, swap(b))
        o_ref[0, HALF:, cols] = jnp.where(low_half, swap(a), b)

    loop(0, NZ - 1, lambda i: kv_copy(far(i), z).wait_send())
    loop(0, NZ, lambda i: x_copy(i, xh).wait_send())
    loop(1, 16, lambda i: h_copy(lax.rem(grp + i, 16), grp).wait_send())
    loop(0, NZ - 1, lambda i: q_copy(far(i), z).wait_send())
    loop(0, NZ - 1, lambda i: o_copy(far(i), z).wait_send())


def body(queries, keys, values, hist_keys, hist_values, lengths, hist_mask):
    hbm = pl.BlockSpec(memory_space=pl.ANY)
    smem = pl.BlockSpec(memory_space=pltpu.SMEM)
    dma = pltpu.SemaphoreType.DMA
    vmem = pltpu.VMEM
    ch = HEADS * HD
    return pl.pallas_call(
        kernel,
        out_shape=jax.ShapeDtypeStruct((1, TOK, ch), BF),
        in_specs=[hbm] * 5 + [smem] * 2,
        out_specs=pl.BlockSpec(memory_space=pltpu.VMEM),
        scratch_shapes=[
            vmem((TOK, ch), BF), vmem((TOK, ch), BF), vmem((TOK, ch), BF),
            vmem((HROWS, TOK), BF), vmem((HROWS, TOK), BF),
            vmem((HEADS, TOK, TOK), BF), vmem((SLOTS, TOK, TOK), BF),
            vmem((HROWS, TOK), BF), vmem((16, HROWS, TOK), BF),
            vmem((NZ, HALF, TOK), BF), vmem((NZ, HALF, TOK), BF),
            vmem((NZ, HALF, TOK), BF), vmem((NZ, HALF, TOK), BF),
            vmem((KEYS, TOK), BF), vmem((KEYS, TOK), BF),
            vmem((2 * TOK, KEYS), jnp.float32),
            dma((5,)), *[dma((16,))] * 10,
        ],
        compiler_params=pltpu.CompilerParams(
            collective_id=0, has_side_effects=True, vmem_limit_bytes=48 * 2**20
        ),
        cost_estimate=pl.CostEstimate(
            flops=4 * 2048 * KEYS * HD, bytes_accessed=2**20, transcendentals=2048 * KEYS
        ),
    )(queries, keys, values, hist_keys, hist_values, lengths, hist_mask)


def solution(mesh):
    return jax.shard_map(
        body,
        mesh=mesh,
        in_specs=(
            P("grp", "seq", None),
            P("grp", "seq", None),
            P("grp", "seq", None),
            P("grp", None),
            P("grp", None),
            P("grp"),
            P("grp", None),
        ),
        out_specs=P("grp", "seq", None),
        check_vma=False,
    )
```

```python
import jax
import jax.numpy as jnp
from jax import lax
from jax.experimental import pallas as pl
from jax.experimental.pallas import tpu as pltpu
from jax.sharding import PartitionSpec as P

HD = 64
HEADS = 16
NZ = 16
TOK = 128
HALF = TOK // 2
SLOTS = 32
HROWS = 64
HIST = 1024
OWN = NZ * TOK
FIRST = OWN + HIST
KEYS = OWN + FIRST
AHEAD = 4
DEAD = -1e30
WINDOW = 8
MESH = pl.DeviceIdType.MESH
BF = jnp.bfloat16


def swap(x):
    return pltpu.roll(x, HD, 1)


def kernel(
    q_hbm, k_hbm, v_hbm, hk_hbm, hv_hbm, len_hbm, mask_hbm, o_ref,
    q_in, k_in, v_in, hk_in, hv_in,
    kv_src, kv_all, h_all, q_src, q_all, o_src, o_all,
    k2, v2, s_ref, acc_ref, top_ref, len_ref, mask_ref,
    in_sem, kv_rs, x_rs, h_rs, q_rs, kv_ss, x_ss, h_ss, q_ss, o_ss, o_rs,
):
    grp = lax.axis_index("grp")
    seq = lax.axis_index("seq")
    z = seq // 2
    xh = lax.rem(seq, 2)
    hcol = pl.multiple_of(z // 2 * TOK, TOK)
    odd = lax.rem(z, 2)

    loads = [
        pltpu.make_async_copy(k_hbm.at[0], k_in, in_sem.at[0]),
        pltpu.make_async_copy(v_hbm.at[0], v_in, in_sem.at[1]),
        pltpu.make_async_copy(hk_hbm.at[:, pl.ds(hcol, TOK)], hk_in, in_sem.at[2]),
        pltpu.make_async_copy(hv_hbm.at[:, pl.ds(hcol, TOK)], hv_in, in_sem.at[3]),
        pltpu.make_async_copy(q_hbm.at[0], q_in, in_sem.at[4]),
        pltpu.make_async_copy(len_hbm, len_ref, in_sem.at[5]),
        pltpu.make_async_copy(mask_hbm, mask_ref, in_sem.at[6]),
    ]
    for load in loads:
        load.start()

    def z_peer(t):
        return {"seq": t * 2 + xh}

    barrier = pltpu.get_barrier_semaphore()

    def far(i):
        return lax.rem(z + 8 + (1 - 2 * lax.rem(i, 2)) * ((i + 1) // 2), NZ)

    def greet_z(i, c):
        pl.semaphore_signal(barrier, inc=1, device_id=z_peer(far(i)), device_id_type=MESH)
        return c

    lax.fori_loop(0, NZ - 1, greet_z, 0)
    pl.semaphore_signal(barrier, inc=1, device_id={"seq": z * 2 + 1 - xh}, device_id_type=MESH)

    y = grp // 4
    pair = grp + 1 - 2 * lax.rem(grp, 2)
    side = grp + 2 - 4 * lax.rem(grp // 2, 2)

    def y_peer(i):
        return lax.rem(grp + 4 * i, 16)

    for peer in (pair, side, y_peer(1), y_peer(2), y_peer(3)):
        pl.semaphore_signal(barrier, inc=1, device_id={"grp": peer}, device_id_type=MESH)

    def lane(rows):
        return lax.broadcasted_iota(jnp.int32, (rows, TOK), 1)

    low = lane(TOK) < HD
    low_half = lane(HALF) < HD

    loads[0].wait()
    loads[1].wait()
    for c in range(HEADS // 2):
        kk = k_in[:, c * TOK : (c + 1) * TOK]
        vv = v_in[:, c * TOK : (c + 1) * TOK]
        kv_src[2 * c] = jnp.where(low, kk, swap(vv))
        kv_src[2 * c + 1] = jnp.where(low, swap(kk), vv)
    loads[2].wait()
    loads[3].wait()
    hk = hk_in[...]
    hv = hv_in[...]
    even_h = jnp.where(low_half, hk, swap(hv))
    odd_h = jnp.where(low_half, swap(hk), hv)
    pick = jnp.full((HROWS, TOK), odd, jnp.int32) == 1
    h_all[grp] = jnp.where(pick, odd_h, even_h)

    pl.semaphore_wait(barrier, 21)

    def kv_copy(t, slot):
        return pltpu.make_async_remote_copy(
            src_ref=kv_src.at[t], dst_ref=kv_all.at[slot * 2 + xh],
            send_sem=kv_ss, recv_sem=kv_rs.at[slot],
            device_id=z_peer(t), device_id_type=MESH,
        )

    def x_copy(t, side):
        return pltpu.make_async_remote_copy(
            src_ref=kv_all.at[t * 2 + side], dst_ref=kv_all.at[t * 2 + side],
            send_sem=x_ss, recv_sem=x_rs.at[t],
            device_id={"seq": z * 2 + 1 - xh}, device_id_type=MESH,
        )

    def h_copy(peer, base, count, recv):
        part = h_all.at[pl.ds(base, count)]
        return pltpu.make_async_remote_copy(
            src_ref=part, dst_ref=part, send_sem=h_ss, recv_sem=h_rs.at[recv],
            device_id={"grp": peer}, device_id_type=MESH,
        )

    two = grp // 2 * 2
    h_sends = [h_copy(pair, grp, 1, 0), h_copy(side, two, 2, 1)]
    h_sends += [h_copy(y_peer(i), y * 4, 4, 1 + i) for i in (1, 2, 3)]
    h_recvs = [h_copy(pair, pair, 1, 0), h_copy(side, side // 2 * 2, 2, 1)]
    h_recvs += [h_copy(y_peer(i), y_peer(4 - i) // 4 * 4, 4, 1 + i) for i in (1, 2, 3)]

    def q_copy(t, slot):
        return pltpu.make_async_remote_copy(
            src_ref=q_src.at[t], dst_ref=q_all.at[slot],
            send_sem=q_ss, recv_sem=q_rs.at[slot],
            device_id=z_peer(t), device_id_type=MESH,
        )

    def o_copy(t, slot):
        return pltpu.make_async_remote_copy(
            src_ref=o_src.at[t], dst_ref=o_all.at[slot],
            send_sem=o_ss, recv_sem=o_rs,
            device_id=z_peer(t), device_id_type=MESH,
        )

    def loop(lo, hi, f):
        def step(i, c):
            f(i)
            return c

        lax.fori_loop(lo, hi, step, 0)

    loop(0, WINDOW, lambda i: kv_copy(far(i), z).start())
    kv_all[z * 2 + xh] = kv_src[z]
    x_copy(z, xh).start()
    h_sends[0].start()

    loads[4].wait()
    scale = jnp.asarray(HD**-0.5, BF)
    for c in range(HEADS // 2):
        qq = q_in[:, c * TOK : (c + 1) * TOK] * scale
        top, bot = qq[:HALF], qq[HALF:]
        q_src[2 * c] = jnp.where(low_half, top, swap(bot))
        q_src[2 * c + 1] = jnp.where(low_half, swap(top), bot)
    q_all[z] = q_src[z]
    q_copy(lax.rem(z + 12, NZ), z).start()
    loop(9, 15, lambda i: q_copy(far(i), z).start())
    h_recvs[0].wait_recv()
    h_sends[1].start()

    loads[5].wait()
    loads[6].wait()
    length = len_ref[0]

    def prepare(rows, at, live):
        column = lane(rows)
        k2[pl.ds(at, rows), :] = jnp.where((column == HD) & jnp.logical_not(live), DEAD, 0.0).astype(BF)
        v2[pl.ds(at, rows), :] = jnp.where(column == HD, 1.0, 0.0).astype(BF)

    def prepare_own(t, side_x, base):
        pos = (t * 2 + side_x) * TOK + lax.broadcasted_iota(jnp.int32, (TOK, TOK), 0)
        prepare(TOK, pl.multiple_of(base + t * TOK, TOK), pos < length)

    def prepare_both(t):
        prepare_own(t, xh, 0)
        prepare_own(t, 1 - xh, FIRST)

    loop(0, NZ, prepare_both)
    for b in range(HIST // TOK):
        prepare(TOK, OWN + b * TOK, jnp.full((TOK, TOK), mask_ref[0, b], jnp.int32) > 0)

    def place(kv, rows, at):
        k2[pl.ds(at, rows), :HD] = kv[:, :HD]
        v2[pl.ds(at, rows), :HD] = kv[:, HD:]

    def place_own(t, side_x, base):
        place(kv_all[t * 2 + side_x], TOK, pl.multiple_of(base + t * TOK, TOK))

    place_own(z, xh, 0)
    h_recvs[1].wait_recv()
    for send in h_sends[2:]:
        send.start()

    def on_kv(i):
        t = far(i)
        kv_copy(t, t).wait_recv()
        x_copy(t, xh).start()

        @pl.when(i < NZ - 1 - WINDOW)
        def _():
            kv_copy(far(i + WINDOW), z).start()

        @pl.when(i >= 7)
        def _():
            q_copy(far(i - 7), z).start()

        place_own(t, xh, 0)

    loop(0, NZ - 1, on_kv)

    for recv in h_recvs[2:]:
        recv.wait_recv()
    for b in range(16):
        place(h_all[b], HROWS, OWN + b * HROWS)

    def open_q(t):
        packed = q_all[t]
        one = jnp.where(lane(HALF) == HD, 1.0, 0.0).astype(BF)
        return [jnp.where(low_half, packed, one), jnp.where(low_half, swap(packed), one)]

    def close_o(rows):
        return jnp.where(low_half, rows[:HALF], swap(rows[HALF:]))

    rows = 2 * TOK
    chunk = 1024

    def sources(j):
        away = jnp.where(j < 3, j + 1, jnp.where(j == 3, 4, jnp.where(j == 4, 7, jnp.where(j == 5, 8, 11 - j + 1))))
        first = lax.rem(z + away, NZ)
        second = jnp.where(j == 3, z, jnp.where(j == 5, lax.rem(z + 12, NZ), lax.rem(z + NZ - away, NZ)))
        return first, second

    def query_rows(j):
        first, second = sources(j)
        return jnp.concatenate(open_q(first) + open_q(second), axis=0)

    def wait_q(j):
        first, second = sources(j)
        q_copy(first, first).wait_recv()

        @pl.when(j != 3)
        def _():
            q_copy(second, second).wait_recv()

    def part(q2, lo, hi):
        best = jnp.full((rows, TOK), -jnp.inf, jnp.float32)
        for c in range(lo, hi, chunk):
            scores = lax.dot_general(
                q2, k2[c : c + chunk, :], (((1,), (1,)), ((), ())), preferred_element_type=jnp.float32
            )
            s_ref[:, c : c + chunk] = scores
            for n in range(0, chunk, TOK):
                best = jnp.maximum(best, scores[:, n : n + TOK])
        top = jnp.max(best, axis=1, keepdims=True)
        mixed = jnp.zeros((rows, TOK), jnp.float32)
        for c in range(lo, hi, chunk):
            weights = jnp.exp(s_ref[:, c : c + chunk] - top).astype(BF)
            mixed += jnp.dot(weights, v2[c : c + chunk, :], preferred_element_type=jnp.float32)
        return mixed, top

    def finish(j, mixed):
        first, second = sources(j)
        out = (mixed / mixed[:, HD : HD + 1]).astype(BF)
        o_src[first] = close_o(out[:TOK])
        o_copy(first, z).start()

        @pl.when(j == 3)
        def _():
            o_all[z] = close_o(out[TOK:])

        @pl.when(j != 3)
        def _():
            o_src[second] = close_o(out[TOK:])
            o_copy(second, z).start()

    def begin(j):
        wait_q(j)
        mixed, top = part(query_rows(j), 0, FIRST)
        acc_ref[j] = mixed
        top_ref[j] = jnp.broadcast_to(top, (rows, TOK))

    loop(0, AHEAD, begin)

    x_copy(z, 1 - xh).wait_recv()
    place_own(z, 1 - xh, FIRST)

    def on_x(i):
        t = far(i)
        x_copy(t, 1 - xh).wait_recv()
        place_own(t, 1 - xh, FIRST)

    loop(0, NZ - 1, on_x)

    def merge(j):
        mixed, top = part(query_rows(j), FIRST, KEYS)
        before = top_ref[j]
        both = jnp.maximum(before, top)
        finish(j, acc_ref[j] * jnp.exp(before - both) + mixed * jnp.exp(top - both))

    def whole(j):
        wait_q(j)
        mixed, top = part(query_rows(j), 0, KEYS)
        finish(j, mixed)

    loop(AHEAD, 8, whole)
    loop(0, AHEAD, lambda i: merge(jnp.where(i < 2, 2 + i, 3 - i)))

    arrived = o_all.at[pl.ds(0, NZ - 1)]
    pltpu.make_async_remote_copy(
        src_ref=arrived, dst_ref=arrived, send_sem=o_ss, recv_sem=o_rs,
        device_id=z_peer(far(0)), device_id_type=MESH,
    ).wait_recv()
    for c in range(HEADS // 2):
        a, b = o_all[2 * c], o_all[2 * c + 1]
        cols = slice(c * TOK, (c + 1) * TOK)
        o_ref[0, :HALF, cols] = jnp.where(low_half, a, swap(b))
        o_ref[0, HALF:, cols] = jnp.where(low_half, swap(a), b)

    def drain(ref, count, sem):
        part = ref.at[pl.ds(0, count)]
        pltpu.make_async_remote_copy(
            src_ref=part, dst_ref=part, send_sem=sem, recv_sem=o_rs,
            device_id=z_peer(far(0)), device_id_type=MESH,
        ).wait_send()

    drain(kv_src, NZ - 1, kv_ss)
    drain(kv_all, NZ, x_ss)
    drain(h_all, 15, h_ss)
    drain(q_src, NZ - 1, q_ss)
    drain(o_src, NZ - 1, o_ss)


def body(queries, keys, values, hist_keys, hist_values, lengths, hist_mask):
    hbm = pl.BlockSpec(memory_space=pl.ANY)
    smem = pltpu.SMEM
    dma = pltpu.SemaphoreType.DMA
    vmem = pltpu.VMEM
    ch = HEADS * HD
    return pl.pallas_call(
        kernel,
        out_shape=jax.ShapeDtypeStruct((1, TOK, ch), BF),
        in_specs=[hbm] * 7,
        out_specs=pl.BlockSpec(memory_space=pltpu.VMEM),
        scratch_shapes=[
            vmem((TOK, ch), BF), vmem((TOK, ch), BF), vmem((TOK, ch), BF),
            vmem((HROWS, TOK), BF), vmem((HROWS, TOK), BF),
            vmem((HEADS, TOK, TOK), BF), vmem((SLOTS, TOK, TOK), BF),
            vmem((16, HROWS, TOK), BF),
            vmem((NZ, HALF, TOK), BF), vmem((NZ, HALF, TOK), BF),
            vmem((NZ, HALF, TOK), BF), vmem((NZ, HALF, TOK), BF),
            vmem((KEYS, TOK), BF), vmem((KEYS, TOK), BF),
            vmem((2 * TOK, KEYS), jnp.float32),
            vmem((AHEAD, 2 * TOK, TOK), jnp.float32), vmem((AHEAD, 2 * TOK, TOK), jnp.float32),
            smem((1,), jnp.int32), smem((1, 8), jnp.int32),
            dma((7,)), dma((16,)), dma((16,)), dma((5,)), dma((16,)), *[dma(())] * 6,
        ],
        compiler_params=pltpu.CompilerParams(
            collective_id=0, has_side_effects=True, vmem_limit_bytes=63 * 2**20
        ),
        cost_estimate=pl.CostEstimate(
            flops=4 * 2048 * KEYS * HD, bytes_accessed=2**20, transcendentals=2048 * KEYS
        ),
    )(queries, keys, values, hist_keys, hist_values, lengths, hist_mask)


def solution(mesh):
    return jax.shard_map(
        body,
        mesh=mesh,
        in_specs=(
            P("grp", "seq", None),
            P("grp", "seq", None),
            P("grp", "seq", None),
            P("grp", None),
            P("grp", None),
            P("grp"),
            P("grp", None),
        ),
        out_specs=P("grp", "seq", None),
        check_vma=False,
    )
```

```python
import jax
import jax.numpy as jnp
from jax import lax
from jax.experimental import pallas as pl
from jax.experimental.pallas import tpu as pltpu
from jax.sharding import PartitionSpec as P

HD = 64
HEADS = 16
NZ = 16
TOK = 128
HALF = TOK // 2
SLOTS = 32
HROWS = 64
HIST = 1024
OWN = NZ * TOK
FIRST = OWN + HIST
KEYS = OWN + FIRST
AHEAD = 4
DEAD = -1e30
WINDOW = 8
MESH = pl.DeviceIdType.MESH
BF = jnp.bfloat16


def swap(x):
    return pltpu.roll(x, HD, 1)


def kernel(
    q_hbm, k_hbm, v_hbm, hk_hbm, hv_hbm, len_hbm, mask_hbm, o_all,
    q_in, k_in, v_in, hk_in, hv_in,
    kv_src, kv_all, h_all, q_src, q_all, o_src,
    k2, v2, s_ref, acc_ref, top_ref, len_ref, mask_ref,
    in_sem, kv_rs, x_rs, h_rs, q_rs, kv_ss, x_ss, h_ss, q_ss, o_ss, o_rs,
):
    grp = lax.axis_index("grp")
    seq = lax.axis_index("seq")
    z = seq // 2
    xh = lax.rem(seq, 2)
    hcol = pl.multiple_of(z // 2 * TOK, TOK)
    odd = lax.rem(z, 2)

    loads = [
        pltpu.make_async_copy(k_hbm.at[0], k_in, in_sem.at[0]),
        pltpu.make_async_copy(v_hbm.at[0], v_in, in_sem.at[1]),
        pltpu.make_async_copy(hk_hbm.at[:, pl.ds(hcol, TOK)], hk_in, in_sem.at[2]),
        pltpu.make_async_copy(hv_hbm.at[:, pl.ds(hcol, TOK)], hv_in, in_sem.at[3]),
        pltpu.make_async_copy(q_hbm.at[0], q_in, in_sem.at[4]),
        pltpu.make_async_copy(len_hbm, len_ref, in_sem.at[5]),
        pltpu.make_async_copy(mask_hbm, mask_ref, in_sem.at[6]),
    ]
    for load in loads:
        load.start()

    def z_peer(t):
        return {"seq": t * 2 + xh}

    barrier = pltpu.get_barrier_semaphore()

    def far(i):
        return lax.rem(z + 8 + (1 - 2 * lax.rem(i, 2)) * ((i + 1) // 2), NZ)

    def greet_z(i, c):
        pl.semaphore_signal(barrier, inc=1, device_id=z_peer(far(i)), device_id_type=MESH)
        return c

    lax.fori_loop(0, NZ - 1, greet_z, 0)
    pl.semaphore_signal(barrier, inc=1, device_id={"seq": z * 2 + 1 - xh}, device_id_type=MESH)

    y = grp // 4
    pair = grp + 1 - 2 * lax.rem(grp, 2)
    side = grp + 2 - 4 * lax.rem(grp // 2, 2)

    def y_peer(i):
        return lax.rem(grp + 4 * i, 16)

    for peer in (pair, side, y_peer(1), y_peer(2), y_peer(3)):
        pl.semaphore_signal(barrier, inc=1, device_id={"grp": peer}, device_id_type=MESH)

    def lane(rows):
        return lax.broadcasted_iota(jnp.int32, (rows, TOK), 1)

    low = lane(TOK) < HD
    low_half = lane(HALF) < HD

    loads[0].wait()
    loads[1].wait()
    for c in range(HEADS // 2):
        kk = k_in[:, c * TOK : (c + 1) * TOK]
        vv = v_in[:, c * TOK : (c + 1) * TOK]
        kv_src[2 * c] = jnp.where(low, kk, swap(vv))
        kv_src[2 * c + 1] = jnp.where(low, swap(kk), vv)
    loads[2].wait()
    loads[3].wait()
    hk = hk_in[...]
    hv = hv_in[...]
    even_h = jnp.where(low_half, hk, swap(hv))
    odd_h = jnp.where(low_half, swap(hk), hv)
    pick = jnp.full((HROWS, TOK), odd, jnp.int32) == 1
    h_all[grp] = jnp.where(pick, odd_h, even_h)

    pl.semaphore_wait(barrier, 21)

    def kv_copy(t, slot):
        return pltpu.make_async_remote_copy(
            src_ref=kv_src.at[t], dst_ref=kv_all.at[slot * 2 + xh],
            send_sem=kv_ss, recv_sem=kv_rs.at[slot],
            device_id=z_peer(t), device_id_type=MESH,
        )

    def x_copy(t, side):
        return pltpu.make_async_remote_copy(
            src_ref=kv_all.at[t * 2 + side], dst_ref=kv_all.at[t * 2 + side],
            send_sem=x_ss, recv_sem=x_rs.at[t],
            device_id={"seq": z * 2 + 1 - xh}, device_id_type=MESH,
        )

    def h_copy(peer, base, count, recv):
        part = h_all.at[pl.ds(base, count)]
        return pltpu.make_async_remote_copy(
            src_ref=part, dst_ref=part, send_sem=h_ss, recv_sem=h_rs.at[recv],
            device_id={"grp": peer}, device_id_type=MESH,
        )

    two = grp // 2 * 2
    h_sends = [h_copy(pair, grp, 1, 0), h_copy(side, two, 2, 1)]
    h_sends += [h_copy(y_peer(i), y * 4, 4, 1 + i) for i in (1, 2, 3)]
    h_recvs = [h_copy(pair, pair, 1, 0), h_copy(side, side // 2 * 2, 2, 1)]
    h_recvs += [h_copy(y_peer(i), y_peer(4 - i) // 4 * 4, 4, 1 + i) for i in (1, 2, 3)]

    def q_copy(t, slot):
        return pltpu.make_async_remote_copy(
            src_ref=q_src.at[t], dst_ref=q_all.at[slot],
            send_sem=q_ss, recv_sem=q_rs.at[slot],
            device_id=z_peer(t), device_id_type=MESH,
        )

    def o_copy(t, slot):
        return pltpu.make_async_remote_copy(
            src_ref=o_src.at[t], dst_ref=o_all.at[slot],
            send_sem=o_ss, recv_sem=o_rs,
            device_id=z_peer(t), device_id_type=MESH,
        )

    def loop(lo, hi, f):
        def step(i, c):
            f(i)
            return c

        lax.fori_loop(lo, hi, step, 0)

    loop(0, WINDOW, lambda i: kv_copy(far(i), z).start())
    kv_all[z * 2 + xh] = kv_src[z]
    x_copy(z, xh).start()
    h_sends[0].start()

    loads[4].wait()
    scale = jnp.asarray(HD**-0.5, BF)
    for c in range(HEADS // 2):
        qq = q_in[:, c * TOK : (c + 1) * TOK] * scale
        top, bot = qq[:HALF], qq[HALF:]
        q_src[2 * c] = jnp.where(low_half, top, swap(bot))
        q_src[2 * c + 1] = jnp.where(low_half, swap(top), bot)
    q_all[z] = q_src[z]
    q_copy(lax.rem(z + 12, NZ), z).start()
    loop(9, 15, lambda i: q_copy(far(i), z).start())
    h_recvs[0].wait_recv()
    h_sends[1].start()

    loads[5].wait()
    loads[6].wait()
    length = len_ref[0]

    def prepare(rows, at, live):
        column = lane(rows)
        k2[pl.ds(at, rows), :] = jnp.where((column == HD) & jnp.logical_not(live), DEAD, 0.0).astype(BF)
        v2[pl.ds(at, rows), :] = jnp.where(column == HD, 1.0, 0.0).astype(BF)

    def prepare_own(t, side_x, base):
        pos = (t * 2 + side_x) * TOK + lax.broadcasted_iota(jnp.int32, (TOK, TOK), 0)
        prepare(TOK, pl.multiple_of(base + t * TOK, TOK), pos < length)

    def prepare_both(t):
        prepare_own(t, xh, 0)
        prepare_own(t, 1 - xh, FIRST)

    loop(0, NZ, prepare_both)
    for b in range(HIST // TOK):
        prepare(TOK, OWN + b * TOK, jnp.full((TOK, TOK), mask_ref[0, b], jnp.int32) > 0)

    def place(kv, rows, at):
        k2[pl.ds(at, rows), :HD] = kv[:, :HD]
        v2[pl.ds(at, rows), :HD] = kv[:, HD:]

    def place_own(t, side_x, base):
        place(kv_all[t * 2 + side_x], TOK, pl.multiple_of(base + t * TOK, TOK))

    place_own(z, xh, 0)
    h_recvs[1].wait_recv()
    for send in h_sends[2:]:
        send.start()

    def on_kv(i):
        t = far(i)
        kv_copy(t, t).wait_recv()
        x_copy(t, xh).start()

        @pl.when(i < NZ - 1 - WINDOW)
        def _():
            kv_copy(far(i + WINDOW), z).start()

        @pl.when(i >= 7)
        def _():
            q_copy(far(i - 7), z).start()

        place_own(t, xh, 0)

    loop(0, NZ - 1, on_kv)

    for recv in h_recvs[2:]:
        recv.wait_recv()
    for b in range(16):
        place(h_all[b], HROWS, OWN + b * HROWS)

    def open_q(t):
        packed = q_all[t]
        one = jnp.where(lane(HALF) == HD, 1.0, 0.0).astype(BF)
        return [jnp.where(low_half, packed, one), jnp.where(low_half, swap(packed), one)]

    def close_o(rows):
        return jnp.where(low_half, rows[:HALF], swap(rows[HALF:]))

    rows = 2 * TOK
    chunk = 1024

    def sources(j):
        away = jnp.where(j < 3, j + 1, jnp.where(j == 3, 4, jnp.where(j == 4, 7, jnp.where(j == 5, 8, 11 - j + 1))))
        first = lax.rem(z + away, NZ)
        second = jnp.where(j == 3, z, jnp.where(j == 5, lax.rem(z + 12, NZ), lax.rem(z + NZ - away, NZ)))
        return first, second

    def query_rows(j):
        first, second = sources(j)
        return jnp.concatenate(open_q(first) + open_q(second), axis=0)

    def wait_q(j):
        first, second = sources(j)
        q_copy(first, first).wait_recv()

        @pl.when(j != 3)
        def _():
            q_copy(second, second).wait_recv()

    def part(q2, lo, hi):
        best = jnp.full((rows, TOK), -jnp.inf, jnp.float32)
        for c in range(lo, hi, chunk):
            scores = lax.dot_general(
                q2, k2[c : c + chunk, :], (((1,), (1,)), ((), ())), preferred_element_type=jnp.float32
            )
            s_ref[:, c : c + chunk] = scores
            for n in range(0, chunk, TOK):
                best = jnp.maximum(best, scores[:, n : n + TOK])
        top = jnp.max(best, axis=1, keepdims=True)
        mixed = jnp.zeros((rows, TOK), jnp.float32)
        for c in range(lo, hi, chunk):
            weights = jnp.exp(s_ref[:, c : c + chunk] - top).astype(BF)
            mixed += jnp.dot(weights, v2[c : c + chunk, :], preferred_element_type=jnp.float32)
        return mixed, top

    own_out = pltpu.make_async_copy(o_src.at[z], o_all.at[z], in_sem.at[7])

    def finish(j, mixed):
        first, second = sources(j)
        out = (mixed / mixed[:, HD : HD + 1]).astype(BF)
        o_src[first] = close_o(out[:TOK])
        o_copy(first, z).start()

        @pl.when(j == 3)
        def _():
            o_src[z] = close_o(out[TOK:])
            own_out.start()

        @pl.when(j != 3)
        def _():
            o_src[second] = close_o(out[TOK:])
            o_copy(second, z).start()

    def begin(j):
        wait_q(j)
        mixed, top = part(query_rows(j), 0, FIRST)
        acc_ref[j] = mixed
        top_ref[j] = jnp.broadcast_to(top, (rows, TOK))

    loop(0, AHEAD, begin)

    x_copy(z, 1 - xh).wait_recv()
    place_own(z, 1 - xh, FIRST)

    def on_x(i):
        t = far(i)
        x_copy(t, 1 - xh).wait_recv()
        place_own(t, 1 - xh, FIRST)

    loop(0, NZ - 1, on_x)

    def merge(j):
        mixed, top = part(query_rows(j), FIRST, KEYS)
        before = top_ref[j]
        both = jnp.maximum(before, top)
        finish(j, acc_ref[j] * jnp.exp(before - both) + mixed * jnp.exp(top - both))

    def whole(j):
        wait_q(j)
        mixed, top = part(query_rows(j), 0, KEYS)
        finish(j, mixed)

    def answer(i):
        @pl.when((i < 1) | (i > 4))
        def _():
            merge(jnp.where(i < 1, 2, jnp.where(i == 5, 3, 7 - i)))

        @pl.when((i >= 1) & (i <= 4))
        def _():
            whole(i + 3)

    loop(0, 8, answer)

    arrived = o_all.at[pl.ds(0, NZ - 1)]
    pltpu.make_async_remote_copy(
        src_ref=arrived, dst_ref=arrived, send_sem=o_ss, recv_sem=o_rs,
        device_id=z_peer(far(0)), device_id_type=MESH,
    ).wait_recv()
    own_out.wait()

    def drain(ref, count, sem):
        part = ref.at[pl.ds(0, count)]
        pltpu.make_async_remote_copy(
            src_ref=part, dst_ref=part, send_sem=sem, recv_sem=o_rs,
            device_id=z_peer(far(0)), device_id_type=MESH,
        ).wait_send()

    drain(kv_src, NZ - 1, kv_ss)
    drain(kv_all, NZ, x_ss)
    drain(h_all, 15, h_ss)
    drain(q_src, NZ - 1, q_ss)
    drain(o_src, NZ - 1, o_ss)


def unpack(slot_ref, o_ref):
    low = lax.broadcasted_iota(jnp.int32, (HALF, TOK), 1) < HD
    for c in range(slot_ref.shape[0] // 2):
        a, b = slot_ref[2 * c], slot_ref[2 * c + 1]
        cols = slice(c * TOK, (c + 1) * TOK)
        o_ref[0, :HALF, cols] = jnp.where(low, a, swap(b))
        o_ref[0, HALF:, cols] = jnp.where(low, swap(a), b)


def body(queries, keys, values, hist_keys, hist_values, lengths, hist_mask):
    hbm = pl.BlockSpec(memory_space=pl.ANY)
    smem = pltpu.SMEM
    dma = pltpu.SemaphoreType.DMA
    vmem = pltpu.VMEM
    ch = HEADS * HD
    slots = pl.pallas_call(
        kernel,
        out_shape=jax.ShapeDtypeStruct((NZ, HALF, TOK), BF),
        in_specs=[hbm] * 7,
        out_specs=hbm,
        scratch_shapes=[
            vmem((TOK, ch), BF), vmem((TOK, ch), BF), vmem((TOK, ch), BF),
            vmem((HROWS, TOK), BF), vmem((HROWS, TOK), BF),
            vmem((HEADS, TOK, TOK), BF), vmem((SLOTS, TOK, TOK), BF),
            vmem((16, HROWS, TOK), BF),
            vmem((NZ, HALF, TOK), BF), vmem((NZ, HALF, TOK), BF), vmem((NZ, HALF, TOK), BF),
            vmem((KEYS, TOK), BF), vmem((KEYS, TOK), BF),
            vmem((2 * TOK, KEYS), jnp.float32),
            vmem((AHEAD, 2 * TOK, TOK), jnp.float32), vmem((AHEAD, 2 * TOK, TOK), jnp.float32),
            smem((1,), jnp.int32), smem((1, 8), jnp.int32),
            dma((8,)), dma((16,)), dma((16,)), dma((5,)), dma((16,)), *[dma(())] * 6,
        ],
        compiler_params=pltpu.CompilerParams(
            collective_id=0, has_side_effects=True, vmem_limit_bytes=63 * 2**20
        ),
        cost_estimate=pl.CostEstimate(
            flops=4 * 2048 * KEYS * HD, bytes_accessed=2**20, transcendentals=2048 * KEYS
        ),
    )(queries, keys, values, hist_keys, hist_values, lengths, hist_mask)
    parts = 2
    return pl.pallas_call(
        unpack,
        grid=(parts,),
        out_shape=jax.ShapeDtypeStruct((1, TOK, ch), BF),
        in_specs=[pl.BlockSpec((NZ // parts, HALF, TOK), lambda i: (i, 0, 0))],
        out_specs=pl.BlockSpec((1, TOK, ch // parts), lambda i: (0, 0, i)),
        compiler_params=pltpu.CompilerParams(vmem_limit_bytes=63 * 2**20),
    )(slots)


def solution(mesh):
    return jax.shard_map(
        body,
        mesh=mesh,
        in_specs=(
            P("grp", "seq", None),
            P("grp", "seq", None),
            P("grp", "seq", None),
            P("grp", None),
            P("grp", None),
            P("grp"),
            P("grp", None),
        ),
        out_specs=P("grp", "seq", None),
        check_vma=False,
    )
```

```python
import jax
import jax.numpy as jnp
from jax import lax
from jax.experimental import pallas as pl
from jax.experimental.pallas import tpu as pltpu
from jax.sharding import PartitionSpec as P

HD = 64
HEADS = 16
NZ = 16
TOK = 128
HALF = TOK // 2
SLOTS = 32
HROWS = 64
HIST = 1024
OWN = NZ * TOK
FIRST = OWN + HIST
KEYS = OWN + FIRST
AHEAD = 4
DEAD = -1e30
WINDOW = 8
MESH = pl.DeviceIdType.MESH
BF = jnp.bfloat16


def swap(x):
    return pltpu.roll(x, HD, 1)


def kernel(
    q_hbm, k_hbm, v_hbm, hk_hbm, hv_hbm, len_hbm, mask_hbm, o_all,
    q_in, k_in, v_in, hk_in, hv_in,
    kv_src, kv_all, h_all, q_src, q_all, o_src,
    k2, v2, s_ref, acc_ref, top_ref, len_ref, mask_ref,
    in_sem, kv_rs, x_rs, h_rs, q_rs, kv_ss, x_ss, h_ss, q_ss, o_ss, o_rs,
):
    grp = lax.axis_index("grp")
    seq = lax.axis_index("seq")
    z = seq // 2
    xh = lax.rem(seq, 2)
    hcol = pl.multiple_of(z // 2 * TOK, TOK)
    odd = lax.rem(z, 2)

    loads = [
        pltpu.make_async_copy(k_hbm.at[0], k_in, in_sem.at[0]),
        pltpu.make_async_copy(v_hbm.at[0], v_in, in_sem.at[1]),
        pltpu.make_async_copy(hk_hbm.at[:, pl.ds(hcol, TOK)], hk_in, in_sem.at[2]),
        pltpu.make_async_copy(hv_hbm.at[:, pl.ds(hcol, TOK)], hv_in, in_sem.at[3]),
        pltpu.make_async_copy(q_hbm.at[0], q_in, in_sem.at[4]),
        pltpu.make_async_copy(len_hbm, len_ref, in_sem.at[5]),
        pltpu.make_async_copy(mask_hbm, mask_ref, in_sem.at[6]),
    ]
    for load in loads:
        load.start()

    def z_peer(t):
        return {"seq": t * 2 + xh}

    barrier = pltpu.get_barrier_semaphore()

    def far(i):
        return lax.rem(z + 8 + (1 - 2 * lax.rem(i, 2)) * ((i + 1) // 2), NZ)

    def greet_z(i, c):
        pl.semaphore_signal(barrier, inc=1, device_id=z_peer(far(i)), device_id_type=MESH)
        return c

    lax.fori_loop(0, NZ - 1, greet_z, 0)
    pl.semaphore_signal(barrier, inc=1, device_id={"seq": z * 2 + 1 - xh}, device_id_type=MESH)

    y = grp // 4
    pair = grp + 1 - 2 * lax.rem(grp, 2)
    side = grp + 2 - 4 * lax.rem(grp // 2, 2)

    def y_peer(i):
        return lax.rem(grp + 4 * i, 16)

    for peer in (pair, side, y_peer(1), y_peer(2), y_peer(3)):
        pl.semaphore_signal(barrier, inc=1, device_id={"grp": peer}, device_id_type=MESH)

    def lane(rows):
        return lax.broadcasted_iota(jnp.int32, (rows, TOK), 1)

    low = lane(TOK) < HD
    low_half = lane(HALF) < HD

    loads[0].wait()
    loads[1].wait()
    for c in range(HEADS // 2):
        kk = k_in[:, c * TOK : (c + 1) * TOK]
        vv = v_in[:, c * TOK : (c + 1) * TOK]
        kv_src[2 * c] = jnp.where(low, kk, swap(vv))
        kv_src[2 * c + 1] = jnp.where(low, swap(kk), vv)
    loads[2].wait()
    loads[3].wait()
    hk = hk_in[...]
    hv = hv_in[...]
    even_h = jnp.where(low_half, hk, swap(hv))
    odd_h = jnp.where(low_half, swap(hk), hv)
    pick = jnp.full((HROWS, TOK), odd, jnp.int32) == 1
    h_all[grp] = jnp.where(pick, odd_h, even_h)

    pl.semaphore_wait(barrier, 21)

    def kv_copy(t, slot):
        return pltpu.make_async_remote_copy(
            src_ref=kv_src.at[t], dst_ref=kv_all.at[slot * 2 + xh],
            send_sem=kv_ss, recv_sem=kv_rs.at[slot],
            device_id=z_peer(t), device_id_type=MESH,
        )

    def x_copy(t, side):
        return pltpu.make_async_remote_copy(
            src_ref=kv_all.at[t * 2 + side], dst_ref=kv_all.at[t * 2 + side],
            send_sem=x_ss, recv_sem=x_rs.at[t],
            device_id={"seq": z * 2 + 1 - xh}, device_id_type=MESH,
        )

    def h_copy(peer, base, count, recv):
        part = h_all.at[pl.ds(base, count)]
        return pltpu.make_async_remote_copy(
            src_ref=part, dst_ref=part, send_sem=h_ss, recv_sem=h_rs.at[recv],
            device_id={"grp": peer}, device_id_type=MESH,
        )

    two = grp // 2 * 2
    h_sends = [h_copy(pair, grp, 1, 0), h_copy(side, two, 2, 1)]
    h_sends += [h_copy(y_peer(i), y * 4, 4, 1 + i) for i in (1, 2, 3)]
    h_recvs = [h_copy(pair, pair, 1, 0), h_copy(side, side // 2 * 2, 2, 1)]
    h_recvs += [h_copy(y_peer(i), y_peer(4 - i) // 4 * 4, 4, 1 + i) for i in (1, 2, 3)]

    def q_copy(t, slot):
        return pltpu.make_async_remote_copy(
            src_ref=q_src.at[t], dst_ref=q_all.at[slot],
            send_sem=q_ss, recv_sem=q_rs.at[slot],
            device_id=z_peer(t), device_id_type=MESH,
        )

    def o_copy(t, slot):
        return pltpu.make_async_remote_copy(
            src_ref=o_src.at[t], dst_ref=o_all.at[slot],
            send_sem=o_ss, recv_sem=o_rs,
            device_id=z_peer(t), device_id_type=MESH,
        )

    def loop(lo, hi, f):
        def step(i, c):
            f(i)
            return c

        lax.fori_loop(lo, hi, step, 0)

    loop(0, WINDOW, lambda i: kv_copy(far(i), z).start())
    kv_all[z * 2 + xh] = kv_src[z]
    x_copy(z, xh).start()
    h_sends[0].start()

    loads[4].wait()
    scale = jnp.asarray(HD**-0.5, BF)
    for c in range(HEADS // 2):
        qq = q_in[:, c * TOK : (c + 1) * TOK] * scale
        top, bot = qq[:HALF], qq[HALF:]
        q_src[2 * c] = jnp.where(low_half, top, swap(bot))
        q_src[2 * c + 1] = jnp.where(low_half, swap(top), bot)
    q_all[z] = q_src[z]
    q_copy(lax.rem(z + 12, NZ), z).start()
    loop(9, 15, lambda i: q_copy(far(i), z).start())
    h_recvs[0].wait_recv()
    h_sends[1].start()

    loads[5].wait()
    loads[6].wait()
    length = len_ref[0]

    def prepare(rows, at, live):
        column = lane(rows)
        k2[pl.ds(at, rows), :] = jnp.where((column == HD) & jnp.logical_not(live), DEAD, 0.0).astype(BF)
        v2[pl.ds(at, rows), :] = jnp.where(column == HD, 1.0, 0.0).astype(BF)

    def prepare_own(t, side_x, base):
        pos = (t * 2 + side_x) * TOK + lax.broadcasted_iota(jnp.int32, (TOK, TOK), 0)
        prepare(TOK, pl.multiple_of(base + t * TOK, TOK), pos < length)

    loop(0, NZ, lambda t: prepare_own(t, xh, 0))

    def place(kv, rows, at):
        k2[pl.ds(at, rows), :HD] = kv[:, :HD]
        v2[pl.ds(at, rows), :HD] = kv[:, HD:]

    def place_own(t, side_x, base):
        place(kv_all[t * 2 + side_x], TOK, pl.multiple_of(base + t * TOK, TOK))

    place_own(z, xh, 0)
    h_recvs[1].wait_recv()
    for send in h_sends[2:]:
        send.start()

    def on_kv(i):
        t = far(i)
        kv_copy(t, t).wait_recv()
        x_copy(t, xh).start()

        @pl.when(i < NZ - 1 - WINDOW)
        def _():
            kv_copy(far(i + WINDOW), z).start()

        @pl.when(i >= 7)
        def _():
            q_copy(far(i - 7), z).start()

        place_own(t, xh, 0)
        prepare_own(t, 1 - xh, FIRST)

    prepare_own(z, 1 - xh, FIRST)
    loop(0, 7, on_kv)
    for recv in h_recvs[2:]:
        recv.wait_recv()
    for b in range(HIST // TOK):
        prepare(TOK, OWN + b * TOK, jnp.full((TOK, TOK), mask_ref[0, b], jnp.int32) > 0)
    for b in range(16):
        place(h_all[b], HROWS, OWN + b * HROWS)
    loop(7, NZ - 1, on_kv)

    def open_q(t):
        packed = q_all[t]
        one = jnp.where(lane(HALF) == HD, 1.0, 0.0).astype(BF)
        return [jnp.where(low_half, packed, one), jnp.where(low_half, swap(packed), one)]

    def close_o(rows):
        return jnp.where(low_half, rows[:HALF], swap(rows[HALF:]))

    rows = 2 * TOK
    chunk = 1024

    def sources(j):
        away = jnp.where(j < 3, j + 1, jnp.where(j == 3, 4, jnp.where(j == 4, 7, jnp.where(j == 5, 8, 11 - j + 1))))
        first = lax.rem(z + away, NZ)
        second = jnp.where(j == 3, z, jnp.where(j == 5, lax.rem(z + 12, NZ), lax.rem(z + NZ - away, NZ)))
        return first, second

    def query_rows(j):
        first, second = sources(j)
        return jnp.concatenate(open_q(first) + open_q(second), axis=0)

    def wait_q(j):
        first, second = sources(j)
        q_copy(first, first).wait_recv()

        @pl.when(j != 3)
        def _():
            q_copy(second, second).wait_recv()

    def part(q2, lo, hi):
        best = jnp.full((rows, TOK), -jnp.inf, jnp.float32)
        for c in range(lo, hi, chunk):
            scores = lax.dot_general(
                q2, k2[c : c + chunk, :], (((1,), (1,)), ((), ())), preferred_element_type=jnp.float32
            )
            s_ref[:, c : c + chunk] = scores
            for n in range(0, chunk, TOK):
                best = jnp.maximum(best, scores[:, n : n + TOK])
        top = jnp.max(best, axis=1, keepdims=True)
        mixed = jnp.zeros((rows, TOK), jnp.float32)
        for c in range(lo, hi, chunk):
            weights = jnp.exp(s_ref[:, c : c + chunk] - top).astype(BF)
            mixed += jnp.dot(weights, v2[c : c + chunk, :], preferred_element_type=jnp.float32)
        return mixed, top

    own_out = pltpu.make_async_copy(o_src.at[z], o_all.at[z], in_sem.at[7])

    def finish(j, mixed):
        first, second = sources(j)
        out = (mixed / mixed[:, HD : HD + 1]).astype(BF)
        o_src[first] = close_o(out[:TOK])
        o_copy(first, z).start()

        @pl.when(j == 3)
        def _():
            o_src[z] = close_o(out[TOK:])
            own_out.start()

        @pl.when(j != 3)
        def _():
            o_src[second] = close_o(out[TOK:])
            o_copy(second, z).start()

    def begin(j):
        wait_q(j)
        mixed, top = part(query_rows(j), 0, FIRST)
        acc_ref[j] = mixed
        top_ref[j] = jnp.broadcast_to(top, (rows, TOK))

    loop(0, AHEAD, begin)

    x_copy(z, 1 - xh).wait_recv()
    place_own(z, 1 - xh, FIRST)

    def on_x(i):
        t = far(i)
        x_copy(t, 1 - xh).wait_recv()
        place_own(t, 1 - xh, FIRST)

    loop(0, NZ - 1, on_x)

    def merge(j):
        mixed, top = part(query_rows(j), FIRST, KEYS)
        before = top_ref[j]
        both = jnp.maximum(before, top)
        finish(j, acc_ref[j] * jnp.exp(before - both) + mixed * jnp.exp(top - both))

    def whole(j):
        wait_q(j)
        mixed, top = part(query_rows(j), 0, KEYS)
        finish(j, mixed)

    def answer(i):
        @pl.when((i < 1) | (i > 4))
        def _():
            merge(jnp.where(i < 1, 2, jnp.where(i == 5, 3, 7 - i)))

        @pl.when((i >= 1) & (i <= 4))
        def _():
            whole(i + 3)

    loop(0, 8, answer)

    arrived = o_all.at[pl.ds(0, NZ - 1)]
    pltpu.make_async_remote_copy(
        src_ref=arrived, dst_ref=arrived, send_sem=o_ss, recv_sem=o_rs,
        device_id=z_peer(far(0)), device_id_type=MESH,
    ).wait_recv()
    own_out.wait()

    def drain(ref, count, sem):
        part = ref.at[pl.ds(0, count)]
        pltpu.make_async_remote_copy(
            src_ref=part, dst_ref=part, send_sem=sem, recv_sem=o_rs,
            device_id=z_peer(far(0)), device_id_type=MESH,
        ).wait_send()

    drain(kv_src, NZ - 1, kv_ss)
    drain(kv_all, NZ, x_ss)
    drain(h_all, 15, h_ss)
    drain(q_src, NZ - 1, q_ss)
    drain(o_src, NZ - 1, o_ss)


def unpack(slot_ref, o_ref):
    low = lax.broadcasted_iota(jnp.int32, (HALF, TOK), 1) < HD
    for c in range(slot_ref.shape[0] // 2):
        a, b = slot_ref[2 * c], slot_ref[2 * c + 1]
        cols = slice(c * TOK, (c + 1) * TOK)
        o_ref[0, :HALF, cols] = jnp.where(low, a, swap(b))
        o_ref[0, HALF:, cols] = jnp.where(low, swap(a), b)


def body(queries, keys, values, hist_keys, hist_values, lengths, hist_mask):
    hbm = pl.BlockSpec(memory_space=pl.ANY)
    smem = pltpu.SMEM
    dma = pltpu.SemaphoreType.DMA
    vmem = pltpu.VMEM
    ch = HEADS * HD
    slots = pl.pallas_call(
        kernel,
        out_shape=jax.ShapeDtypeStruct((NZ, HALF, TOK), BF),
        in_specs=[hbm] * 7,
        out_specs=hbm,
        scratch_shapes=[
            vmem((TOK, ch), BF), vmem((TOK, ch), BF), vmem((TOK, ch), BF),
            vmem((HROWS, TOK), BF), vmem((HROWS, TOK), BF),
            vmem((HEADS, TOK, TOK), BF), vmem((SLOTS, TOK, TOK), BF),
            vmem((16, HROWS, TOK), BF),
            vmem((NZ, HALF, TOK), BF), vmem((NZ, HALF, TOK), BF), vmem((NZ, HALF, TOK), BF),
            vmem((KEYS, TOK), BF), vmem((KEYS, TOK), BF),
            vmem((2 * TOK, KEYS), jnp.float32),
            vmem((AHEAD, 2 * TOK, TOK), jnp.float32), vmem((AHEAD, 2 * TOK, TOK), jnp.float32),
            smem((1,), jnp.int32), smem((1, 8), jnp.int32),
            dma((8,)), dma((16,)), dma((16,)), dma((5,)), dma((16,)), *[dma(())] * 6,
        ],
        compiler_params=pltpu.CompilerParams(
            collective_id=0, has_side_effects=True, vmem_limit_bytes=63 * 2**20
        ),
        cost_estimate=pl.CostEstimate(
            flops=4 * 2048 * KEYS * HD, bytes_accessed=2**20, transcendentals=2048 * KEYS
        ),
    )(queries, keys, values, hist_keys, hist_values, lengths, hist_mask)
    parts = 2
    return pl.pallas_call(
        unpack,
        grid=(parts,),
        out_shape=jax.ShapeDtypeStruct((1, TOK, ch), BF),
        in_specs=[pl.BlockSpec((NZ // parts, HALF, TOK), lambda i: (i, 0, 0))],
        out_specs=pl.BlockSpec((1, TOK, ch // parts), lambda i: (0, 0, i)),
        compiler_params=pltpu.CompilerParams(vmem_limit_bytes=63 * 2**20),
    )(slots)


def solution(mesh):
    return jax.shard_map(
        body,
        mesh=mesh,
        in_specs=(
            P("grp", "seq", None),
            P("grp", "seq", None),
            P("grp", "seq", None),
            P("grp", None),
            P("grp", None),
            P("grp"),
            P("grp", None),
        ),
        out_specs=P("grp", "seq", None),
        check_vma=False,
    )
```
